256 devices in a mesh: dp: 8 (over y, core), tensor: 32 (over x, z).
Axes of the slice: x: 4, y: 4, z: 8, core: 2. Of those that a mesh axis runs over, the one named last changes fastest.
Arguments:
- activations: bfloat16 [65536, 8192], P(('dp', 'tensor')), may hold values from -6 to 6
- cotangent: bfloat16 [65536, 1024], P(('dp', 'tensor')), may hold values from -6 to 6
- frozen_weight: bfloat16 [8192, 1024], P('tensor'), may hold values from -0.0625 to 0.0625
- adapter_down: bfloat16 [12, 8192, 64], P(None, 'tensor'), may hold values from -0.0625 to 0.0625
- adapter_up: bfloat16 [12, 64, 1024], replicated, may hold values from -0.75 to 0.75
- held_jobs: int32 [8, 3], P('dp'), may hold values from 0 to 11, as said below
- tile_slots: int32 [512], P(('dp', 'tensor')), may hold values from 0 to 2
- tile_lengths: int32 [512], P(('dp', 'tensor')), may hold values from 16 to 128
Outputs:
- grad_input: bfloat16 [65536, 8192], P(('dp', 'tensor'))
- grad_down: float32 [12, 8192, 64], P(None, 'tensor')
- grad_up: float32 [12, 64, 1024], replicated
The draws below stay inside these ranges and needn't reach their ends.
Inputs may be any that keep to these rules, and one draw needn't show every extreme that they name: `held_jobs`: each row lists 3 different adapters, and every adapter appears in some row.
All inputs are finite; a program needn't handle non-finite values.
Results may differ from the reference program's by a relative error of at most 0.0046.
Values may be sent and summed in bfloat16 or wider, within the bound.
No kernel may reach another device: no remote copies, remote signals or barrier semaphores. Data moves between devices by JAX's collectives and lax.ppermute only.
A program may use at most 128 MiB of HBM per device.

```python
import math
import jax
import jax.numpy as jnp
import numpy as np
from jax import lax

D = 8192
DV = 1024
R = 64
JOBS = 12
HELD = 3
TILE = 128
TOK_DEV = 256
TOKENS = 65536
TILES = 512
N_DP = 8
N_TENSOR = 32


def draw_held_jobs(key, part):
    key = jax.random.fold_in(key, 11)
    copies = (N_DP * HELD + JOBS - 1) // JOBS
    orders = [jax.random.permutation(jax.random.fold_in(key, number), JOBS) for number in range(copies)]
    return jnp.concatenate(orders)[:N_DP * HELD].reshape(N_DP, HELD).astype(jnp.int32)


def draw_tile_lengths(key, part):
    key = jax.random.fold_in(key, 12)
    return jnp.minimum(jax.random.randint(key, (TILES,), 16, 192), 128).astype(jnp.int32)


def touch_ends(entries, stream_key, low, high):
    longest = entries.shape.index(max(entries.shape))
    spots = []
    for shift in (0, 1):
        where = [jax.random.randint(jax.random.fold_in(stream_key, axis), (), 0, length) for axis, length in enumerate(entries.shape)]
        where[longest] = (where[longest] + shift) % entries.shape[longest]
        spots.append(tuple(where))
    return entries.at[spots[0]].set(low).at[spots[1]].set(high)


def steps_of(key, extent, pieces, smallest, high):
    level = 1.0
    for axis_at, parts in pieces:
        steps = jax.random.uniform(jax.random.fold_in(jax.random.fold_in(key, 6), axis_at), (parts,), jnp.float32, smallest / len(pieces), high / len(pieces))
        level = level * jnp.repeat(jnp.exp(steps), extent[axis_at] // parts).reshape((-1,) + (1,) * (len(extent) - 1 - axis_at))
    return level


def rank_bounds(count, slope):
    portions = [(1 << 20) // math.isqrt(standing ** slope) + 1 for standing in range(1, count + 1)]
    width = 1 + sum(portions) // (1 << 30)
    return np.cumsum(np.array([max(1, weight // width) for weight in portions]))


def ranked(stream_key, extent, number_of, slope):
    table = rank_bounds(number_of, slope)
    lot = jax.random.randint(jax.random.fold_in(stream_key, 1), extent, 0, int(table[number_of - 1]))
    grade = jnp.searchsorted(jnp.asarray(table, jnp.int32), lot, side="right")
    return jax.random.permutation(jax.random.fold_in(stream_key, 2), number_of)[grade].astype(jnp.int32)


def noise(key, dims, scale, bound, shards=(), kind=jnp.bfloat16):
    drawn = jax.random.normal(key, dims, jnp.float32) * scale
    if len(shards) > 0:
        drawn = steps_of(key, dims, shards, -0.22, 0.18) * drawn
    return jnp.clip(drawn, min=-bound, max=bound).astype(kind)


def setup_inputs(seed: int = 0) -> dict:
    keys = jax.random.split(jax.random.key(seed), 9)
    activations = noise(keys[0], (TOKENS, D), 1.0, 6.0, ((0, 256),))
    cotangent = noise(keys[1], (TOKENS, DV), 1.0, 6.0, ((0, 256),))
    frozen_weight = noise(keys[2], (D, DV), D ** -0.5, 0.0625, ((0, 32),))
    adapter_down = noise(keys[3], (JOBS, D, R), D ** -0.5, 0.0625, ((1, 32),))
    adapter_up = noise(keys[4], (JOBS, R, DV), R ** -0.5, 0.75)
    held_jobs = draw_held_jobs(jax.random.fold_in(keys[8], 71), 0)
    tile_slots = touch_ends(ranked(keys[6], (TILES,), HELD, 2), jax.random.fold_in(keys[6], 3), 0, HELD - 1).astype(jnp.int32)
    tile_lengths = draw_tile_lengths(jax.random.fold_in(keys[8], 71), 0)
    return dict(activations=activations, cotangent=cotangent, frozen_weight=frozen_weight, adapter_down=adapter_down, adapter_up=adapter_up, held_jobs=held_jobs, tile_slots=tile_slots, tile_lengths=tile_lengths)


ADAPTER_SCALING = 2.0


def reference(activations, cotangent, frozen_weight, adapter_down, adapter_up, held_jobs, tile_slots, tile_lengths):
    tiles_group = TOK_DEV * N_TENSOR // TILE
    tile_ids = jnp.arange(TILES, dtype=jnp.int32)
    tile_jobs = held_jobs[(tile_ids // tiles_group).astype(jnp.int32), tile_slots]
    positions = jnp.arange(TILE, dtype=jnp.int32)
    live_mask = (positions[None, :] < tile_lengths[:, None]).astype(jnp.bfloat16)
    masked = cotangent.reshape(TILES, TILE, DV) * live_mask[:, :, None]
    block = 16
    rounds = TILES // block
    inputs_all = activations.reshape(rounds, block, TILE, D)
    grads_all = masked.reshape(rounds, block, TILE, DV)
    jobs_all = tile_jobs.reshape(rounds, block)
    job_ids = jnp.arange(JOBS, dtype=jnp.int32)
    highest_precision = lax.Precision.HIGHEST

    def advance(totals, inputs_now):
        summed_down_gradient, summed_up_gradient = totals
        tokens_blk, grads_blk, jobs_blk = inputs_now
        selected_down_weight = adapter_down[jobs_blk].astype(jnp.float32)
        up_sel = adapter_up[jobs_blk].astype(jnp.float32)
        tokens_f = tokens_blk.astype(jnp.float32)
        grads_f = grads_blk.astype(jnp.float32)
        low_rank = jnp.einsum('tkd,tdr->tkr', tokens_f, selected_down_weight, precision=highest_precision).astype(jnp.bfloat16)
        back_rank = jnp.einsum('tkv,trv->tkr', grads_f, up_sel, precision=highest_precision).astype(jnp.bfloat16)
        low_f = low_rank.astype(jnp.float32)
        backward_function = back_rank.astype(jnp.float32)
        adapter_input_gradient = ADAPTER_SCALING * jnp.einsum('gfy,gey->gfe', backward_function, selected_down_weight, precision=highest_precision)
        frozen = jnp.dot(grads_blk.reshape(block * TILE, DV), frozen_weight.T, preferred_element_type=jnp.float32)
        grad_input = (frozen + adapter_input_gradient.reshape(block * TILE, D)).astype(jnp.bfloat16)
        job_selector_matrix = (jobs_blk[:, None] == job_ids[None, :]).astype(jnp.float32)
        tile_down_gradient = jnp.einsum('tkd,tkr->tdr', tokens_f, backward_function, precision=highest_precision)
        tile_up_gradient = jnp.einsum('tkr,tkv->trv', low_f, grads_f, precision=highest_precision)
        summed_down_gradient = summed_down_gradient + ADAPTER_SCALING * jnp.einsum('ea,eow->aow', job_selector_matrix, tile_down_gradient, precision=highest_precision)
        summed_up_gradient = summed_up_gradient + ADAPTER_SCALING * jnp.einsum('ce,cqm->eqm', job_selector_matrix, tile_up_gradient, precision=highest_precision)
        return (summed_down_gradient, summed_up_gradient), grad_input

    start = (jnp.zeros((JOBS, D, R), jnp.float32), jnp.zeros((JOBS, R, DV), jnp.float32))
    (grad_down, grad_up), grad_input = lax.scan(advance, start, (inputs_all, grads_all, jobs_all))
    return grad_input.reshape(TOKENS, D), grad_down, grad_up
```

```python
import jax
import jax.numpy as jnp
from jax import lax
from jax.sharding import Mesh, PartitionSpec as P

ADAPTER_SCALING = 2.0
NY, NCORE, NX, NZ = 4, 2, 4, 8
SWAP = [(0, 1), (1, 0)]


def shift(value, axis, size, by):
    return lax.ppermute(value, axis, [(i, (i + by) % size) for i in range(size)])


def ring_gather(block, axis, size, me):
    rows, columns = block.shape
    half = columns // 2
    whole = jnp.zeros((rows, size * columns), block.dtype)

    def put(whole, piece, owner, offset):
        return lax.dynamic_update_slice(whole, piece, (0, owner * columns + offset))

    whole = put(whole, block, me, 0)
    right = left = block
    for step in range(1, size // 2):
        right = shift(right, axis, size, 1)
        left = shift(left, axis, size, -1)
        whole = put(whole, right, (me - step) % size, 0)
        whole = put(whole, left, (me + step) % size, 0)
    far = (me + size // 2) % size
    whole = put(whole, shift(right[:, :half], axis, size, 1), far, 0)
    whole = put(whole, shift(left[:, half:], axis, size, -1), far, half)
    return whole


def exchange(pick, axis, size, me):
    got = [pick(me)]
    for by in range(1, size):
        got.append(shift(pick((me + by) % size), axis, size, by))
    return got


def body(activations, cotangent, frozen_weight, adapter_down, adapter_up, held_jobs, tile_slots, tile_lengths):
    f32, bf16 = jnp.float32, jnp.bfloat16
    rows, width = activations.shape
    value_width = cotangent.shape[1]
    tiles = tile_slots.shape[0]
    tile_rows = rows // tiles
    jobs, rank = adapter_up.shape[0], adapter_up.shape[1]
    share = adapter_down.shape[1]
    held = held_jobs[0]
    slots = held.shape[0]
    core, x, z = lax.axis_index("core"), lax.axis_index("x"), lax.axis_index("z")

    half = value_width // NCORE
    with jax.named_scope("frozen_gather"):
        own_half = lax.dynamic_slice_in_dim(frozen_weight, core * half, half, 1)
        own_weight = lax.all_gather(own_half, ("x", "z"), axis=0, tiled=True)
        other_weight = lax.ppermute(own_weight, "core", SWAP)

    with jax.named_scope("down_gather"):
        down_mine = jnp.swapaxes(adapter_down, 1, 2)[held].reshape(slots * rank, share)
        down_z = ring_gather(down_mine, "z", NZ, z)
        down_all = ring_gather(down_z, "x", NX, x)

    positions = jnp.arange(tile_rows, dtype=jnp.int32)
    live = (positions[None, :] < tile_lengths[:, None]).astype(bf16).reshape(rows, 1)
    masked = cotangent * live
    up_held = adapter_up[held].reshape(slots * rank, value_width)

    row_tile = jnp.arange(rows, dtype=jnp.int32) // tile_rows
    row_slot = tile_slots[row_tile]
    slot_onehot = row_slot[:, None] == jnp.arange(slots, dtype=jnp.int32)[None, :]
    in_slot = jnp.repeat(slot_onehot, rank, axis=1)
    in_tile = jnp.repeat(row_tile[:, None] == jnp.arange(tiles, dtype=jnp.int32)[None, :], rank, axis=1)

    def pick_slot(value):
        value = jnp.where(in_slot, value, 0.0).reshape(rows, slots, rank)
        return jnp.sum(value, axis=1).astype(bf16)

    def per_tile(value):
        return jnp.where(in_tile, jnp.tile(value, (1, tiles)), jnp.zeros((), bf16))

    back = pick_slot(
        lax.dot_general(masked, up_held, (((1,), (1,)), ((), ())), preferred_element_type=f32)
    )
    back_slots = jnp.where(in_slot, jnp.tile(back, (1, slots)), jnp.zeros((), bf16))

    down_terms = (
        ADAPTER_SCALING
        * lax.dot_general(per_tile(back), activations, (((0,), (0,)), ((), ())), preferred_element_type=f32)
    ).astype(bf16)

    with jax.named_scope("slots_x"):
        slots_x = exchange(lambda i: tile_slots, "x", NX, x)

    def sum_by_slot(blocks, height):
        out = []
        for slot in range(slots):
            total = 0.0
            for block, ids in zip(blocks, slots_x):
                for tile in range(tiles):
                    part = block[tile * height : (tile + 1) * height].astype(f32)
                    total = total + jnp.where(ids[tile] == slot, part, 0.0)
            out.append(total)
        return jnp.concatenate(out, axis=0)

    def sum_by_job(parts, ids, height):
        out = []
        for job in range(jobs):
            total = 0.0
            for d in range(NY * NCORE):
                for slot in range(slots):
                    part = parts[d, slot * height : (slot + 1) * height].astype(f32)
                    total = total + jnp.where(ids[d, slot] == job, part, 0.0)
            out.append(total)
        return jnp.stack(out)

    held_rows = jnp.broadcast_to(jnp.pad(held, (0, 16 - slots)).astype(bf16)[:, None], (16, share))

    with jax.named_scope("down_x"):
        span = width // NX
        got = exchange(lambda i: lax.dynamic_slice_in_dim(down_terms, i * span, span, 1), "x", NX, x)
        down_slot = sum_by_slot(got, rank).astype(bf16)
    with jax.named_scope("down_z"):
        got = exchange(lambda i: lax.dynamic_slice_in_dim(down_slot, i * share, share, 1), "z", NZ, z)
        down_share = sum(g.astype(f32) for g in got).astype(bf16)
    with jax.named_scope("down_dp"):
        packed = jnp.concatenate([down_share, held_rows], axis=0)
        packed = lax.all_gather(packed, ("y", "core"), axis=0, tiled=False)
        held_all = packed[:, slots * rank : slots * rank + slots, 0].astype(jnp.int32)
        grad_down = jnp.swapaxes(sum_by_job(packed, held_all, rank), 1, 2)

    low = pick_slot(
        lax.dot_general(activations, down_all, (((1,), (1,)), ((), ())), preferred_element_type=f32)
    )
    up_terms = ADAPTER_SCALING * lax.dot_general(
        per_tile(low), masked, (((0,), (0,)), ((), ())), preferred_element_type=f32
    )
    up_terms = up_terms.astype(bf16).reshape(tiles, rank, value_width)
    deep = rank // NX
    lanes = value_width // NZ
    with jax.named_scope("up_x"):
        got = exchange(
            lambda i: lax.dynamic_slice_in_dim(up_terms, i * deep, deep, 1).reshape(tiles * deep, value_width),
            "x", NX, x,
        )
        up_slot = sum_by_slot(got, deep)
    with jax.named_scope("up_z"):
        got = exchange(lambda i: lax.dynamic_slice_in_dim(up_slot, i * lanes, lanes, 1), "z", NZ, z)
        up_share = sum(got)
    with jax.named_scope("up_dp"):
        up_parts = lax.all_gather(up_share, ("y", "core"), axis=0, tiled=False)
        up_job = sum_by_job(up_parts, held_all, deep).astype(bf16)
    with jax.named_scope("up_spread"):
        some = jobs // NCORE
        mine = lax.dynamic_slice_in_dim(up_job, core * some, some, 0).reshape(some * deep, lanes)
        line = jnp.zeros((some * deep, value_width), bf16)
        for by, block in enumerate(exchange(lambda i: mine, "z", NZ, z)):
            line = lax.dynamic_update_slice(line, block, (0, ((z - by) % NZ) * lanes))
        line = line.reshape(some, deep, value_width)
        full = jnp.zeros((some, rank, value_width), bf16)
        for by, block in enumerate(exchange(lambda i: line, "x", NX, x)):
            full = lax.dynamic_update_slice(full, block, (0, ((x - by) % NX) * deep, 0))
        sibling = lax.ppermute(full, "core", SWAP)
        first = jnp.where(core == 0, full, sibling)
        second = jnp.where(core == 0, sibling, full)
        grad_up = jnp.concatenate([first, second], axis=0).astype(f32)

    own_masked = lax.dynamic_slice_in_dim(masked, core * half, half, 1)
    other_masked = lax.dynamic_slice_in_dim(masked, (1 - core) * half, half, 1)
    total = lax.dot_general(own_masked, own_weight, (((1,), (1,)), ((), ())), preferred_element_type=f32)
    total = total + ADAPTER_SCALING * lax.dot_general(
        back_slots, down_all, (((1,), (0,)), ((), ())), preferred_element_type=f32
    )
    total = total + lax.dot_general(
        other_masked, other_weight, (((1,), (1,)), ((), ())), preferred_element_type=f32
    )
    return total.astype(bf16), grad_down, grad_up


def solution(mesh):
    fine = Mesh(mesh.devices.reshape(NY, NCORE, NX, NZ), ("y", "core", "x", "z"))
    dp, tensor, every = ("y", "core"), ("x", "z"), ("y", "core", "x", "z")
    return jax.shard_map(
        body,
        mesh=fine,
        in_specs=(
            P(every, None), P(every, None), P(tensor, None), P(None, tensor, None),
            P(), P(dp, None), P(every), P(every),
        ),
        out_specs=(P(every, None), P(None, tensor, None), P()),
        check_vma=False,
    )
```

```python
import functools
import jax
import jax.numpy as jnp
from jax import lax
from jax.experimental import pallas as pl
from jax.experimental.pallas import tpu as pltpu
from jax.sharding import Mesh, PartitionSpec as P

ADAPTER_SCALING = 2.0
NY, NCORE, NX, NZ = 4, 2, 4, 8
SWAP = [(0, 1), (1, 0)]
PAD = 128
F32, BF16 = jnp.float32, jnp.bfloat16
VMEM = pl.BlockSpec(memory_space=pltpu.VMEM)
SMEM = pl.BlockSpec(memory_space=pltpu.SMEM)
BIG = pltpu.CompilerParams(vmem_limit_bytes=56 * 1024 * 1024)


def shift(value, axis, size, by):
    return lax.ppermute(value, axis, [(i, (i + by) % size) for i in range(size)])


def ring_gather(block, axis, size, me):
    rows, columns = block.shape
    half = columns // 2
    whole = jnp.zeros((rows, size * columns), block.dtype)

    def put(whole, piece, owner, offset):
        return lax.dynamic_update_slice(whole, piece, (0, owner * columns + offset))

    whole = put(whole, block, me, 0)
    right = left = block
    for step in range(1, size // 2):
        right = shift(right, axis, size, 1)
        left = shift(left, axis, size, -1)
        whole = put(whole, right, (me - step) % size, 0)
        whole = put(whole, left, (me + step) % size, 0)
    far = (me + size // 2) % size
    whole = put(whole, shift(right[:, :half], axis, size, 1), far, 0)
    whole = put(whole, shift(left[:, half:], axis, size, -1), far, half)
    return whole


def tn(a, b):
    return lax.dot_general(a, b, (((0,), (0,)), ((), ())), preferred_element_type=F32)


def nt(a, b):
    return lax.dot_general(a, b, (((1,), (1,)), ((), ())), preferred_element_type=F32)


def nn(a, b):
    return lax.dot_general(a, b, (((1,), (0,)), ((), ())), preferred_element_type=F32)


def back_kernel(x, held, slots, lengths, act, cot, up, masked, back_slots, *terms):
    tiles = slots.shape[0]
    tile_rows = cot.shape[0] // tiles
    rank = up.shape[1]
    span = act.shape[1] // NX
    for tile in range(tiles):
        rows = pl.ds(tile * tile_rows, tile_rows)
        slot = slots[tile]
        row = lax.broadcasted_iota(jnp.int32, (tile_rows, 1), 0)
        live = jnp.where(row < lengths[tile], cot[rows, :], jnp.zeros((), BF16))
        masked[rows, :] = live
        back = nt(live, up[held[0, slot]]).astype(BF16)
        twice = back * jnp.asarray(ADAPTER_SCALING, BF16)
        for s in range(held.shape[1]):
            back_slots[rows, s * rank : (s + 1) * rank] = jnp.where(slot == s, twice, jnp.zeros((), BF16))
        ident = jnp.full((rank, PAD), slot.astype(F32), F32).astype(BF16)
        for by, out in enumerate(terms):
            columns = pl.ds(pl.multiple_of(lax.rem(x[0] + by, NX) * span, span), span)
            out[tile * rank : (tile + 1) * rank, :span] = tn(twice, act[rows, columns]).astype(BF16)
            out[tile * rank : (tile + 1) * rank, span:] = ident


def low_kernel(x, slots, act, masked, down, *terms):
    tiles = slots.shape[0]
    tile_rows = act.shape[0] // tiles
    rank = terms[0].shape[0] // tiles * NX
    deep = rank // NX
    for tile in range(tiles):
        rows = pl.ds(tile * tile_rows, tile_rows)
        mine = pl.ds(pl.multiple_of(slots[tile] * rank, rank), rank)
        low = nt(act[rows, :], down[mine, :]).astype(BF16)
        twice = low * jnp.asarray(ADAPTER_SCALING, BF16)
        term = tn(twice, masked[rows, :])
        for owner in range(NX):
            for by, out in enumerate(terms):
                @pl.when(lax.rem(x[0] + by, NX) == owner)
                def _():
                    out[tile * deep : (tile + 1) * deep, :] = term[owner * deep : (owner + 1) * deep, :]


def slot_kernel(slot_count, tiles, *refs):
    downs, ups, out = refs[:NX], refs[NX : 2 * NX], refs[2 * NX]
    rank = downs[0].shape[0] // tiles
    deep = ups[0].shape[0] // tiles
    share = out.shape[2]
    lanes = ups[0].shape[1] // NZ
    span = share * NZ
    idents = [
        [down[tile * rank : (tile + 1) * rank, span : span + PAD].astype(F32) for tile in range(tiles)]
        for down in downs
    ]
    top = slot_count * rank
    half = slot_count * deep // 2
    for z in range(NZ):
        ups_now = []
        for slot in range(slot_count):
            total = jnp.zeros((rank, share), F32)
            some = jnp.zeros((deep, lanes), F32)
            for down, up, ident in zip(downs, ups, idents):
                for tile in range(tiles):
                    part = down[tile * rank : (tile + 1) * rank, z * share : (z + 1) * share].astype(F32)
                    hit = ident[tile] == slot
                    wide = jnp.concatenate([hit] * (share // PAD), axis=1)
                    total = total + jnp.where(wide, part, 0.0)
                    part = up[tile * deep : (tile + 1) * deep, z * lanes : (z + 1) * lanes]
                    some = some + jnp.where(hit[:deep, :lanes], part, 0.0)
            out[z, slot * rank : (slot + 1) * rank, :] = total.astype(BF16)
            ups_now.append(some)
        ups_now = jnp.concatenate(ups_now, axis=0)
        rest = jnp.zeros((out.shape[1] - top - half, share), F32)
        packed = jnp.concatenate([ups_now[:half], ups_now[half:]], axis=1)
        out[z, top:, :] = jnp.concatenate([packed, rest], axis=0).astype(BF16)


def share_kernel(held, parts, out):
    total = parts[0].astype(F32)
    for z in range(1, NZ):
        total = total + parts[z].astype(F32)
    height = out.shape[0]
    row = lax.broadcasted_iota(jnp.int32, total.shape, 0)
    for s in range(held.shape[1]):
        total = jnp.where(row == height - held.shape[1] + s, held[0, s].astype(F32), total)
    out[...] = total.astype(BF16)


def job_kernel(slot_count, core, ids, parts, down, up, acc):
    jobs, rank, _ = down.shape
    deep = acc.shape[1]
    lanes = acc.shape[2]
    top = slot_count * rank
    half = slot_count * deep // 2
    down[...] = jnp.zeros_like(down)
    acc[...] = jnp.zeros_like(acc)
    for d in range(NY * NCORE):
        tail = parts[d, top:, :].astype(F32)
        ups = jnp.concatenate([tail[:half, :lanes], tail[:half, lanes:]], axis=0)
        for slot in range(slot_count):
            job = ids[d, slot]
            down[job] += parts[d, slot * rank : (slot + 1) * rank, :].astype(F32)
            acc[job] += ups[slot * deep : (slot + 1) * deep, :]
    some = jobs // NCORE
    for i in range(some):
        up[i * deep : (i + 1) * deep, :] = acc[core[0] * some + i].astype(BF16)


def spread_kernel(core, mine, other, out):
    some = out.shape[0] // NCORE
    deep = out.shape[1] // NX
    lanes = out.shape[2] // NZ
    for source, which in ((mine, core[0]), (other, 1 - core[0])):
        for i in range(some):
            for x in range(NX):
                row = [source[x, z, i * deep : (i + 1) * deep, :] for z in range(NZ)]
                out[which * some + i, x * deep : (x + 1) * deep, :] = jnp.concatenate(row, axis=1).astype(F32)


def input_kernel(core, masked, own, other, back_slots, down, out):
    half = own.shape[1]
    first = masked[:, :half]
    second = masked[:, half:]
    mine = jnp.where(core[0] == 0, first, second)
    theirs = jnp.where(core[0] == 0, second, first)
    total = nt(mine, own[...]) + nt(theirs, other[...]) + nn(back_slots[...], down[...])
    out[...] = total.astype(BF16)


def body(activations, cotangent, frozen_weight, adapter_down, adapter_up, held_jobs, tile_slots, tile_lengths):
    rows, width = activations.shape
    value_width = cotangent.shape[1]
    tiles = tile_slots.shape[0]
    jobs, rank = adapter_up.shape[0], adapter_up.shape[1]
    share = adapter_down.shape[1]
    held = held_jobs[0]
    slots = held.shape[0]
    span = width // NX
    deep = rank // NX
    lanes = value_width // NZ
    half = value_width // NCORE
    some = jobs // NCORE
    height = -(-(slots * rank + slots * deep // 2 + slots) // 32) * 32
    shape = jax.ShapeDtypeStruct
    core = lax.axis_index("core")
    x = lax.axis_index("x")
    z = lax.axis_index("z")
    core_at, x_at = core.reshape(1), x.reshape(1)

    with jax.named_scope("frozen_gather"):
        own_half = lax.dynamic_slice_in_dim(frozen_weight, core * half, half, 1)
        own_weight = lax.all_gather(own_half, ("x", "z"), axis=0, tiled=True)
        other_weight = lax.ppermute(own_weight, "core", SWAP)

    with jax.named_scope("down_gather"):
        down_mine = jnp.swapaxes(adapter_down, 1, 2)[held].reshape(slots * rank, share)
        down_z = ring_gather(down_mine, "z", NZ, z)
        down_all = ring_gather(down_z, "x", NX, x)

    with jax.named_scope("down_terms"):
        masked, back_slots, *down_terms = pl.pallas_call(
            back_kernel,
            out_shape=[shape((rows, value_width), BF16), shape((rows, slots * rank), BF16)]
            + [shape((tiles * rank, span + PAD), BF16)] * NX,
            in_specs=[SMEM] * 4 + [VMEM] * 3,
            out_specs=[VMEM] * (2 + NX),
            compiler_params=BIG,
        )(x_at, held_jobs, tile_slots, tile_lengths, activations, cotangent, adapter_up)
    with jax.named_scope("down_x"):
        down_got = [term if by == 0 else shift(term, "x", NX, by) for by, term in enumerate(down_terms)]

    with jax.named_scope("up_terms"):
        up_terms = pl.pallas_call(
            low_kernel,
            out_shape=[shape((tiles * deep, value_width), F32)] * NX,
            in_specs=[SMEM] * 2 + [VMEM] * 3,
            out_specs=[VMEM] * NX,
            compiler_params=BIG,
        )(x_at, tile_slots, activations, masked, down_all)
    with jax.named_scope("up_x"):
        up_got = [term if by == 0 else shift(term, "x", NX, by) for by, term in enumerate(up_terms)]

    with jax.named_scope("sum_x"):
        by_z = pl.pallas_call(
            functools.partial(slot_kernel, slots, tiles),
            out_shape=shape((NZ, height, share), BF16),
            in_specs=[VMEM] * (2 * NX),
            out_specs=VMEM,
            compiler_params=BIG,
        )(*down_got, *up_got)
    with jax.named_scope("exchange_z"):
        from_z = lax.all_to_all(by_z, "z", 0, 0, tiled=True)
    with jax.named_scope("sum_z"):
        mine = pl.pallas_call(
            share_kernel,
            out_shape=shape((height, share), BF16),
            in_specs=[SMEM, VMEM],
            out_specs=VMEM,
            compiler_params=BIG,
        )(held_jobs, from_z)
    with jax.named_scope("gather_dp"):
        groups = lax.all_gather(mine, ("y", "core"), axis=0, tiled=False)
        ids = groups[:, height - slots :, 0].astype(jnp.int32)
    with jax.named_scope("sum_dp"):
        grad_down, up_mine = pl.pallas_call(
            functools.partial(job_kernel, slots),
            out_shape=[shape((jobs, rank, share), F32), shape((some * deep, lanes), BF16)],
            in_specs=[SMEM, SMEM, VMEM],
            out_specs=[VMEM, VMEM],
            scratch_shapes=[pltpu.VMEM((jobs, deep, lanes), F32)],
            compiler_params=BIG,
        )(core_at, ids, groups)
        grad_down = jnp.swapaxes(grad_down, 1, 2)
    with jax.named_scope("up_spread"):
        line = lax.all_gather(up_mine, "z", axis=0, tiled=False)
        square = lax.all_gather(line, "x", axis=0, tiled=False)
        sibling = lax.ppermute(square, "core", SWAP)
        grad_up = pl.pallas_call(
            spread_kernel,
            out_shape=shape((jobs, rank, value_width), F32),
            in_specs=[SMEM, VMEM, VMEM],
            out_specs=VMEM,
            compiler_params=BIG,
        )(core_at, square, sibling)

    with jax.named_scope("grad_input"):
        block = 1024
        grad_input = pl.pallas_call(
            input_kernel,
            grid=(width // block,),
            out_shape=shape((rows, width), BF16),
            in_specs=[
                SMEM,
                pl.BlockSpec((rows, value_width), lambda i: (0, 0)),
                pl.BlockSpec((block, half), lambda i: (i, 0)),
                pl.BlockSpec((block, half), lambda i: (i, 0)),
                pl.BlockSpec((rows, slots * rank), lambda i: (0, 0)),
                pl.BlockSpec((slots * rank, block), lambda i: (0, i)),
            ],
            out_specs=pl.BlockSpec((rows, block), lambda i: (0, i)),
            compiler_params=BIG,
        )(core_at, masked, own_weight, other_weight, back_slots, down_all)
    return grad_input, grad_down, grad_up


def solution(mesh):
    fine = Mesh(mesh.devices.reshape(NY, NCORE, NX, NZ), ("y", "core", "x", "z"))
    dp, tensor, every = ("y", "core"), ("x", "z"), ("y", "core", "x", "z")
    return jax.shard_map(
        body,
        mesh=fine,
        in_specs=(
            P(every, None), P(every, None), P(tensor, None), P(None, tensor, None),
            P(), P(dp, None), P(every), P(every),
        ),
        out_specs=(P(every, None), P(None, tensor, None), P()),
        check_vma=False,
    )
```

```python
import functools
import jax
import jax.numpy as jnp
from jax import lax
from jax.experimental import pallas as pl
from jax.experimental.pallas import tpu as pltpu
from jax.sharding import Mesh, PartitionSpec as P

ADAPTER_SCALING = 2.0
NY, NCORE, NX, NZ = 4, 2, 4, 8
SWAP = [(0, 1), (1, 0)]
PAD = 128
F32, BF16 = jnp.float32, jnp.bfloat16
VMEM = pl.BlockSpec(memory_space=pltpu.VMEM)
SMEM = pl.BlockSpec(memory_space=pltpu.SMEM)
BIG = pltpu.CompilerParams(vmem_limit_bytes=56 * 1024 * 1024)


def cost(microseconds):
    return pl.CostEstimate(flops=0, transcendentals=0, bytes_accessed=int(microseconds * 3_000_000))


def shift(value, axis, size, by):
    return lax.ppermute(value, axis, [(i, (i + by) % size) for i in range(size)])


def after(value, event):
    return lax.optimization_barrier((value, event))[0]


def ring_gather(block, axis, size, me, second=None, last=None):
    rows, columns = block.shape
    half = columns // 2
    whole = jnp.zeros((rows, size * columns), block.dtype)

    def put(whole, piece, owner, offset):
        return lax.dynamic_update_slice(whole, piece, (0, owner * columns + offset))

    whole = put(whole, block, me, 0)
    right = left = block
    for step in range(1, size // 2):
        right = shift(right, axis, size, 1)
        left = shift(left, axis, size, -1)
        whole = put(whole, right, (me - step) % size, 0)
        whole = put(whole, left, (me + step) % size, 0)
        if step == 1 and second is not None:
            right, left = after((right, left), second)
    if last is not None:
        right, left = after((right, left), last)
    far = (me + size // 2) % size
    whole = put(whole, shift(right[:, :half], axis, size, 1), far, 0)
    whole = put(whole, shift(left[:, half:], axis, size, -1), far, half)
    return whole


def tn(a, b):
    return lax.dot_general(a, b, (((0,), (0,)), ((), ())), preferred_element_type=F32)


def nt(a, b):
    return lax.dot_general(a, b, (((1,), (1,)), ((), ())), preferred_element_type=F32)


def nn(a, b):
    return lax.dot_general(a, b, (((1,), (0,)), ((), ())), preferred_element_type=F32)


def back_kernel(x, held, slots, lengths, act, cot, up, masked, back_slots, *terms):
    tiles = slots.shape[0]
    tile_rows = cot.shape[0] // tiles
    rank = up.shape[1]
    span = act.shape[1] // NX
    for tile in range(tiles):
        rows = pl.ds(tile * tile_rows, tile_rows)
        slot = slots[tile]
        row = lax.broadcasted_iota(jnp.int32, (tile_rows, 1), 0)
        live = jnp.where(row < lengths[tile], cot[rows, :], jnp.zeros((), BF16))
        masked[rows, :] = live
        back = nt(live, up[held[0, slot]]).astype(BF16)
        twice = back * jnp.asarray(ADAPTER_SCALING, BF16)
        for s in range(held.shape[1]):
            back_slots[rows, s * rank : (s + 1) * rank] = jnp.where(slot == s, twice, jnp.zeros((), BF16))
        ident = jnp.full((rank, PAD), slot.astype(F32), F32).astype(BF16)
        for by, out in enumerate(terms):
            columns = pl.ds(pl.multiple_of(lax.rem(x[0] + by, NX) * span, span), span)
            out[tile * rank : (tile + 1) * rank, :span] = tn(twice, act[rows, columns]).astype(BF16)
            out[tile * rank : (tile + 1) * rank, span:] = ident


def low_kernel(held, slots, act, masked, down, out):
    tiles = slots.shape[0]
    tile_rows = act.shape[0] // tiles
    deep = 2 * NY * NCORE
    rank = NX * deep
    lanes = out.shape[2]
    terms, marks = [], []
    for tile in range(tiles):
        rows = pl.ds(tile * tile_rows, tile_rows)
        mine = pl.ds(pl.multiple_of(slots[tile] * rank, rank), rank)
        low = nt(act[rows, :], down[mine, :]).astype(BF16)
        twice = low * jnp.asarray(ADAPTER_SCALING, BF16)
        terms.append(tn(twice, masked[rows, :]))
        marks.append(jnp.full((2, lanes), held[0, slots[tile]].astype(F32), F32))
    for x in range(NX):
        for z in range(NZ):
            for d in range(NY * NCORE):
                first = x * deep + 2 * d
                cut = [term[first : first + 2, z * lanes : (z + 1) * lanes] for term in terms]
                out[(x * NZ + z) * NY * NCORE + d] = jnp.concatenate(cut + marks, axis=0).astype(BF16)


def up_job_kernel(jobs, downs, parts, out):
    value = parts[...].astype(F32)
    mark = pltpu.roll(value, 4, 1)
    sums = []
    for job in range(jobs):
        total = jnp.sum(jnp.where(mark == job, value, 0.0), axis=0)
        sums.append(total[0:2] + total[2:4])
    sums.append(jnp.zeros((32 - 2 * jobs, value.shape[2]), F32))
    sums = jnp.concatenate(sums, axis=0)
    top = downs.shape[0]
    out[:top, :] = downs[...]
    out[top:, :] = jnp.concatenate([sums[:16], sums[16:]], axis=1).astype(BF16)


def slot_kernel(slot_count, tiles, *refs):
    downs, out = refs[:NX], refs[NX]
    rank = downs[0].shape[0] // tiles
    share = out.shape[2]
    span = share * NZ
    idents = [
        [down[tile * rank : (tile + 1) * rank, span : span + PAD].astype(F32) for tile in range(tiles)]
        for down in downs
    ]
    for z in range(NZ):
        for slot in range(slot_count):
            total = jnp.zeros((rank, share), F32)
            for down, ident in zip(downs, idents):
                for tile in range(tiles):
                    part = down[tile * rank : (tile + 1) * rank, z * share : (z + 1) * share].astype(F32)
                    wide = jnp.concatenate([ident[tile] == slot] * (share // PAD), axis=1)
                    total = total + jnp.where(wide, part, 0.0)
            out[z, slot * rank : (slot + 1) * rank, :] = total.astype(BF16)


def share_kernel(held, parts, out):
    top = parts.shape[1]
    total = parts[0].astype(F32)
    for z in range(1, NZ):
        total = total + parts[z].astype(F32)
    out[:top, :] = total.astype(BF16)
    more = jnp.zeros((out.shape[0] - top, out.shape[1]), F32)
    row = lax.broadcasted_iota(jnp.int32, more.shape, 0)
    for s in range(held.shape[1]):
        more = jnp.where(row == s, held[0, s].astype(F32), more)
    out[top:, :] = more.astype(BF16)


def job_kernel(slot_count, ids, parts, down):
    rank = down.shape[1]
    down[...] = jnp.zeros_like(down)
    for d in range(NY * NCORE):
        for slot in range(slot_count):
            down[ids[d, slot]] += parts[d, slot * rank : (slot + 1) * rank, :].astype(F32)


def spread_kernel(core, mine, other, out):
    some = out.shape[0] // NCORE
    deep = out.shape[1] // NX
    for source, which in ((mine, core[0]), (other, 1 - core[0])):
        for x in range(NX):
            for i in range(some):
                line = [source[x * NZ + z, i * deep : (i + 1) * deep, :] for z in range(NZ)]
                out[which * some + i, x * deep : (x + 1) * deep, :] = jnp.concatenate(line, axis=1).astype(F32)


def input_kernel(masked, weight, back_slots, down, out):
    out[...] = (nt(masked[...], weight[...]) + nn(back_slots[...], down[...])).astype(BF16)


def body(activations, cotangent, frozen_weight, adapter_down, adapter_up, held_jobs, tile_slots, tile_lengths):
    rows, width = activations.shape
    value_width = cotangent.shape[1]
    tiles = tile_slots.shape[0]
    jobs, rank = adapter_up.shape[0], adapter_up.shape[1]
    share = adapter_down.shape[1]
    held = held_jobs[0]
    slots = held.shape[0]
    span = width // NX
    deep = rank // NX
    lanes = value_width // NZ
    some = jobs // NCORE
    shape = jax.ShapeDtypeStruct
    y = lax.axis_index("y")
    core = lax.axis_index("core")
    x = lax.axis_index("x")
    z = lax.axis_index("z")
    core_at, x_at = core.reshape(1), x.reshape(1)

    with jax.named_scope("frozen_gather"):
        part = frozen_weight.shape[0] // (NY * NCORE)
        own_part = lax.dynamic_slice_in_dim(frozen_weight, (y * NCORE + core) * part, part, 0)
        weight = lax.all_gather(own_part, ("x", "z", "y", "core"), axis=0, tiled=True)

    with jax.named_scope("down_terms"):
        masked, back_slots, *down_terms = pl.pallas_call(
            back_kernel,
            out_shape=[shape((rows, value_width), BF16), shape((rows, slots * rank), BF16)]
            + [shape((tiles * rank, span + PAD), BF16)] * NX,
            in_specs=[SMEM] * 4 + [VMEM] * 3,
            out_specs=[VMEM] * (2 + NX),
            compiler_params=BIG, cost_estimate=cost(5.5),
        )(x_at, held_jobs, tile_slots, tile_lengths, activations, cotangent, adapter_up)
    with jax.named_scope("down_x"):
        down_got = [term if by == 0 else shift(term, "x", NX, by) for by, term in enumerate(down_terms)]
    with jax.named_scope("down_sum_x"):
        down_by_z = pl.pallas_call(
            functools.partial(slot_kernel, slots, tiles),
            out_shape=shape((NZ, slots * rank, share), BF16),
            in_specs=[VMEM] * NX,
            out_specs=VMEM,
            compiler_params=BIG, cost_estimate=cost(4),
        )(*down_got)
    with jax.named_scope("down_z"):
        down_from_z = lax.all_to_all(down_by_z, "z", 0, 0, tiled=True)
    with jax.named_scope("down_sum_z"):
        mine = pl.pallas_call(
            share_kernel,
            out_shape=shape((slots * rank + 16, share), BF16),
            in_specs=[SMEM, VMEM],
            out_specs=VMEM,
            compiler_params=BIG, cost_estimate=cost(2),
        )(held_jobs, down_from_z)
    with jax.named_scope("down_gather"):
        down_mine = jnp.swapaxes(adapter_down, 1, 2)[held].reshape(slots * rank, share)
        down_z = ring_gather(down_mine, "z", NZ, z, second=down_terms)
        down_all = ring_gather(after(down_z, down_got), "x", NX, x)

    with jax.named_scope("up_terms"):
        receivers = NX * NZ * NY * NCORE
        up_terms = pl.pallas_call(
            low_kernel,
            out_shape=shape((receivers, 8, lanes), BF16),
            in_specs=[SMEM] * 2 + [VMEM] * 3,
            out_specs=VMEM,
            compiler_params=BIG, cost_estimate=cost(7),
        )(held_jobs, tile_slots, activations, masked, down_all)
    with jax.named_scope("up_all"):
        up_got = lax.all_to_all(up_terms, ("x", "z", "y", "core"), 0, 0, tiled=True)
    with jax.named_scope("up_sum"):
        packed = pl.pallas_call(
            functools.partial(up_job_kernel, jobs),
            out_shape=shape((slots * rank + 32, share), BF16),
            in_specs=[VMEM, VMEM],
            out_specs=VMEM,
            compiler_params=BIG, cost_estimate=cost(3),
        )(mine, up_got)
    with jax.named_scope("gather_dp"):
        groups = lax.all_gather(packed, ("y", "core"), axis=0, tiled=False)
        ids = groups[:, slots * rank : slots * rank + slots, 0].astype(jnp.int32)
    with jax.named_scope("down_dp"):
        grad_down = pl.pallas_call(
            functools.partial(job_kernel, slots),
            out_shape=shape((jobs, rank, share), F32),
            in_specs=[SMEM, VMEM],
            out_specs=VMEM,
            compiler_params=BIG, cost_estimate=cost(2.5),
        )(ids, groups)
    with jax.named_scope("up_spread"):
        ups = groups[:, slots * rank + 16 :]
        ups = jnp.concatenate([ups[:, :, :lanes], ups[:, :, lanes:]], axis=1)[:, : 2 * jobs]
        ups = ups.reshape(NY * NCORE, jobs, 2, lanes).transpose(1, 0, 2, 3)
        ups = lax.dynamic_slice_in_dim(ups, core * some, some, 0).reshape(some * deep, lanes)
        square = lax.all_to_all(jnp.broadcast_to(ups, (NX * NZ,) + ups.shape), ("x", "z"), 0, 0)
    with jax.named_scope("grad_input"):
        block = 1024
        grad_input = pl.pallas_call(
            input_kernel,
            grid=(width // block,),
            out_shape=shape((rows, width), BF16),
            in_specs=[
                pl.BlockSpec((rows, value_width), lambda i: (0, 0)),
                pl.BlockSpec((block, value_width), lambda i: (i, 0)),
                pl.BlockSpec((rows, slots * rank), lambda i: (0, 0)),
                pl.BlockSpec((slots * rank, block), lambda i: (0, i)),
            ],
            out_specs=pl.BlockSpec((rows, block), lambda i: (0, i)),
            compiler_params=BIG, cost_estimate=cost(13),
        )(masked, weight, back_slots, down_all)
    with jax.named_scope("up_swap"):
        sibling = lax.ppermute(after(square, grad_input), "core", SWAP)
        grad_up = pl.pallas_call(
            spread_kernel,
            out_shape=shape((jobs, rank, value_width), F32),
            in_specs=[SMEM, VMEM, VMEM],
            out_specs=VMEM,
            compiler_params=BIG, cost_estimate=cost(3),
        )(core_at, square, sibling)
    return grad_input, jnp.swapaxes(grad_down, 1, 2), grad_up


def solution(mesh):
    fine = Mesh(mesh.devices.reshape(NY, NCORE, NX, NZ), ("y", "core", "x", "z"))
    dp, tensor, every = ("y", "core"), ("x", "z"), ("y", "core", "x", "z")
    return jax.shard_map(
        body,
        mesh=fine,
        in_specs=(
            P(every, None), P(every, None), P(tensor, None), P(None, tensor, None),
            P(), P(dp, None), P(every), P(every),
        ),
        out_specs=(P(every, None), P(None, tensor, None), P()),
        check_vma=False,
    )
```

```python
import functools
import jax
import jax.numpy as jnp
from jax import lax
from jax.experimental import pallas as pl
from jax.experimental.pallas import tpu as pltpu
from jax.sharding import Mesh, PartitionSpec as P

ADAPTER_SCALING = 2.0
NY, NCORE, NX, NZ = 4, 2, 4, 8
SWAP = [(0, 1), (1, 0)]
PAD = 128
F32, BF16 = jnp.float32, jnp.bfloat16
VMEM = pl.BlockSpec(memory_space=pltpu.VMEM)
SMEM = pl.BlockSpec(memory_space=pltpu.SMEM)
BIG = pltpu.CompilerParams(vmem_limit_bytes=56 * 1024 * 1024)


def cost(microseconds):
    return pl.CostEstimate(flops=0, transcendentals=0, bytes_accessed=int(microseconds * 3_000_000))


def shift(value, axis, size, by):
    return lax.ppermute(value, axis, [(i, (i + by) % size) for i in range(size)])


def after(value, event):
    return lax.optimization_barrier((value, event))[0]


def ring_gather(block, axis, size, me, second=None, last=None):
    rows, columns = block.shape
    half = columns // 2
    whole = jnp.zeros((rows, size * columns), block.dtype)

    def put(whole, piece, owner, offset):
        return lax.dynamic_update_slice(whole, piece, (0, owner * columns + offset))

    whole = put(whole, block, me, 0)
    right = left = block
    for step in range(1, size // 2):
        right = shift(right, axis, size, 1)
        left = shift(left, axis, size, -1)
        whole = put(whole, right, (me - step) % size, 0)
        whole = put(whole, left, (me + step) % size, 0)
        if step == 1 and second is not None:
            right, left = after((right, left), second)
    if last is not None:
        right, left = after((right, left), last)
    far = (me + size // 2) % size
    whole = put(whole, shift(right[:, :half], axis, size, 1), far, 0)
    whole = put(whole, shift(left[:, half:], axis, size, -1), far, half)
    return whole


def tn(a, b):
    return lax.dot_general(a, b, (((0,), (0,)), ((), ())), preferred_element_type=F32)


def nt(a, b):
    return lax.dot_general(a, b, (((1,), (1,)), ((), ())), preferred_element_type=F32)


def nn(a, b):
    return lax.dot_general(a, b, (((1,), (0,)), ((), ())), preferred_element_type=F32)


def back_kernel(x, held, slots, lengths, act, cot, up, masked, back_slots, *terms):
    tiles = slots.shape[0]
    tile_rows = cot.shape[0] // tiles
    rank = up.shape[1]
    span = act.shape[1] // NX
    for tile in range(tiles):
        rows = pl.ds(tile * tile_rows, tile_rows)
        slot = slots[tile]
        row = lax.broadcasted_iota(jnp.int32, (tile_rows, 1), 0)
        live = jnp.where(row < lengths[tile], cot[rows, :], jnp.zeros((), BF16))
        masked[rows, :] = live
        back = nt(live, up[held[0, slot]]).astype(BF16)
        twice = back * jnp.asarray(ADAPTER_SCALING, BF16)
        for s in range(held.shape[1]):
            back_slots[rows, s * rank : (s + 1) * rank] = jnp.where(slot == s, twice, jnp.zeros((), BF16))
        ident = jnp.full((rank, PAD), slot.astype(F32), F32).astype(BF16)
        for by, out in enumerate(terms):
            columns = pl.ds(pl.multiple_of(lax.rem(x[0] + by, NX) * span, span), span)
            out[tile * rank : (tile + 1) * rank, :span] = tn(twice, act[rows, columns]).astype(BF16)
            out[tile * rank : (tile + 1) * rank, span:] = ident


def low_kernel(slots, act, masked, down, out):
    tiles = slots.shape[0]
    tile_rows = act.shape[0] // tiles
    lanes = out.shape[2]
    deep = out.shape[1] // tiles - 16
    rank = NX * deep
    terms, marks = [], []
    for tile in range(tiles):
        rows = pl.ds(tile * tile_rows, tile_rows)
        mine = pl.ds(pl.multiple_of(slots[tile] * rank, rank), rank)
        low = nt(act[rows, :], down[mine, :]).astype(BF16)
        twice = low * jnp.asarray(ADAPTER_SCALING, BF16)
        terms.append(tn(twice, masked[rows, :]).astype(BF16))
        marks.append(jnp.full((16, lanes), slots[tile].astype(F32), F32).astype(BF16))
    for to_x in range(NX):
        for to_z in range(NZ):
            for tile in range(tiles):
                cut = terms[tile][to_x * deep : (to_x + 1) * deep, to_z * lanes : (to_z + 1) * lanes]
                out[to_x * NZ + to_z, tile * deep : (tile + 1) * deep, :] = cut
                first = tiles * deep + tile * 16
                out[to_x * NZ + to_z, first : first + 16, :] = marks[tile]


def up_sum_kernel(tiles, deep, held, downs, parts, out):
    slot_count = held.shape[1]
    lanes = parts.shape[2]
    top = downs.shape[0]
    sums = []
    for slot in range(slot_count):
        total = jnp.zeros((deep, lanes), F32)
        for source in range(parts.shape[0]):
            for tile in range(tiles):
                mark = parts[source, tiles * deep + tile * 16 : tiles * deep + (tile + 1) * 16, :].astype(F32)
                part = parts[source, tile * deep : (tile + 1) * deep, :].astype(F32)
                total = total + jnp.where(mark[:deep] == slot, part, 0.0)
        sums.append(total)
    sums = jnp.concatenate(sums, axis=0)
    half = sums.shape[0] // 2
    tail = jnp.concatenate([sums[:half], sums[half:]], axis=1)
    tail = jnp.concatenate([tail, jnp.zeros((out.shape[0] - top - half, out.shape[1]), F32)], axis=0)
    row = lax.broadcasted_iota(jnp.int32, tail.shape, 0)
    for s in range(slot_count):
        tail = jnp.where(row == tail.shape[0] - slot_count + s, held[0, s].astype(F32), tail)
    out[:top, :] = downs[...]
    out[top:, :] = tail.astype(BF16)


def slot_kernel(slot_count, tiles, *refs):
    downs, out = refs[:NX], refs[NX]
    rank = downs[0].shape[0] // tiles
    share = out.shape[2]
    span = share * NZ
    idents = [
        [down[tile * rank : (tile + 1) * rank, span : span + PAD].astype(F32) for tile in range(tiles)]
        for down in downs
    ]
    for z in range(NZ):
        for slot in range(slot_count):
            total = jnp.zeros((rank, share), F32)
            for down, ident in zip(downs, idents):
                for tile in range(tiles):
                    part = down[tile * rank : (tile + 1) * rank, z * share : (z + 1) * share].astype(F32)
                    wide = jnp.concatenate([ident[tile] == slot] * (share // PAD), axis=1)
                    total = total + jnp.where(wide, part, 0.0)
            out[z, slot * rank : (slot + 1) * rank, :] = total.astype(BF16)


def share_kernel(parts, out):
    total = parts[0].astype(F32)
    for z in range(1, NZ):
        total = total + parts[z].astype(F32)
    out[...] = total.astype(BF16)


def job_kernel(slot_count, core, ids, parts, down, up, acc):
    jobs, rank, _ = down.shape
    deep = acc.shape[1]
    lanes = acc.shape[2]
    top = slot_count * rank
    half = slot_count * deep // 2
    down[...] = jnp.zeros_like(down)
    acc[...] = jnp.zeros_like(acc)
    for d in range(NY * NCORE):
        tail = parts[d, top:, :].astype(F32)
        ups = jnp.concatenate([tail[:half, :lanes], tail[:half, lanes:]], axis=0)
        for slot in range(slot_count):
            job = ids[d, slot]
            down[job] += parts[d, slot * rank : (slot + 1) * rank, :].astype(F32)
            acc[job] += ups[slot * deep : (slot + 1) * deep, :]
    some = jobs // NCORE
    for i in range(some):
        mine = acc[core[0] * some + i].astype(BF16)
        for copy in range(up.shape[0]):
            up[copy, i * deep : (i + 1) * deep, :] = mine


def spread_kernel(core, mine, other, out):
    some = out.shape[0] // NCORE
    deep = out.shape[1] // NX
    for source, which in ((mine, core[0]), (other, 1 - core[0])):
        for x in range(NX):
            for i in range(some):
                line = [source[x * NZ + z, i * deep : (i + 1) * deep, :] for z in range(NZ)]
                out[which * some + i, x * deep : (x + 1) * deep, :] = jnp.concatenate(line, axis=1).astype(F32)


def input_kernel(masked, weight, back_slots, down, out):
    out[...] = (nt(masked[...], weight[...]) + nn(back_slots[...], down[...])).astype(BF16)


def body(activations, cotangent, frozen_weight, adapter_down, adapter_up, held_jobs, tile_slots, tile_lengths):
    rows, width = activations.shape
    value_width = cotangent.shape[1]
    tiles = tile_slots.shape[0]
    jobs, rank = adapter_up.shape[0], adapter_up.shape[1]
    share = adapter_down.shape[1]
    held = held_jobs[0]
    slots = held.shape[0]
    span = width // NX
    deep = rank // NX
    lanes = value_width // NZ
    some = jobs // NCORE
    shape = jax.ShapeDtypeStruct
    y = lax.axis_index("y")
    core = lax.axis_index("core")
    x = lax.axis_index("x")
    z = lax.axis_index("z")
    core_at, x_at = core.reshape(1), x.reshape(1)

    with jax.named_scope("frozen_gather"):
        part = frozen_weight.shape[0] // (NY * NCORE)
        own_part = lax.dynamic_slice_in_dim(frozen_weight, (y * NCORE + core) * part, part, 0)
        weight = lax.all_gather(own_part, ("x", "z", "y", "core"), axis=0, tiled=True)

    with jax.named_scope("down_terms"):
        masked, back_slots, *down_terms = pl.pallas_call(
            back_kernel,
            out_shape=[shape((rows, value_width), BF16), shape((rows, slots * rank), BF16)]
            + [shape((tiles * rank, span + PAD), BF16)] * NX,
            in_specs=[SMEM] * 4 + [VMEM] * 3,
            out_specs=[VMEM] * (2 + NX),
            compiler_params=BIG, cost_estimate=cost(5.5),
        )(x_at, held_jobs, tile_slots, tile_lengths, activations, cotangent, adapter_up)
    with jax.named_scope("down_x"):
        down_got = [term if by == 0 else shift(term, "x", NX, by) for by, term in enumerate(down_terms)]
    with jax.named_scope("down_sum_x"):
        down_by_z = pl.pallas_call(
            functools.partial(slot_kernel, slots, tiles),
            out_shape=shape((NZ, slots * rank, share), BF16),
            in_specs=[VMEM] * NX,
            out_specs=VMEM,
            compiler_params=BIG, cost_estimate=cost(4),
        )(*down_got)
    with jax.named_scope("down_z"):
        down_from_z = lax.all_to_all(down_by_z, "z", 0, 0, tiled=True)
    with jax.named_scope("down_sum_z"):
        mine = pl.pallas_call(
            share_kernel,
            out_shape=shape((slots * rank, share), BF16),
            in_specs=[VMEM],
            out_specs=VMEM,
            compiler_params=BIG, cost_estimate=cost(2),
        )(down_from_z)
    with jax.named_scope("down_gather"):
        down_mine = jnp.swapaxes(adapter_down, 1, 2)[held].reshape(slots * rank, share)
        down_z = ring_gather(down_mine, "z", NZ, z, second=down_terms)
        down_all = ring_gather(after(down_z, down_got), "x", NX, x)

    with jax.named_scope("up_terms"):
        up_terms = pl.pallas_call(
            low_kernel,
            out_shape=shape((NX * NZ, tiles * (deep + 16), lanes), BF16),
            in_specs=[SMEM] + [VMEM] * 3,
            out_specs=VMEM,
            compiler_params=BIG, cost_estimate=cost(7),
        )(tile_slots, activations, masked, down_all)
    with jax.named_scope("up_tensor"):
        up_got = lax.all_to_all(up_terms, ("x", "z"), 0, 0, tiled=True)
    with jax.named_scope("up_sum"):
        packed = pl.pallas_call(
            functools.partial(up_sum_kernel, tiles, deep),
            out_shape=shape((slots * rank + 32, share), BF16),
            in_specs=[SMEM, VMEM, VMEM],
            out_specs=VMEM,
            compiler_params=BIG, cost_estimate=cost(2),
        )(held_jobs, mine, up_got)
    with jax.named_scope("gather_dp"):
        groups = lax.all_gather(packed, ("y", "core"), axis=0, tiled=False)
        ids = groups[:, slots * rank + 32 - slots :, 0].astype(jnp.int32)
    with jax.named_scope("sum_dp"):
        grad_down, up_copies = pl.pallas_call(
            functools.partial(job_kernel, slots),
            out_shape=[shape((jobs, rank, share), F32), shape((NX * NZ, some * deep, lanes), BF16)],
            in_specs=[SMEM, SMEM, VMEM],
            out_specs=[VMEM, VMEM],
            scratch_shapes=[pltpu.VMEM((jobs, deep, lanes), F32)],
            compiler_params=BIG, cost_estimate=cost(2.5),
        )(core_at, ids, groups)
    with jax.named_scope("up_spread"):
        square = lax.all_to_all(up_copies, ("x", "z"), 0, 0)
    with jax.named_scope("grad_input"):
        block = 1024
        grad_input = pl.pallas_call(
            input_kernel,
            grid=(width // block,),
            out_shape=shape((rows, width), BF16),
            in_specs=[
                pl.BlockSpec((rows, value_width), lambda i: (0, 0)),
                pl.BlockSpec((block, value_width), lambda i: (i, 0)),
                pl.BlockSpec((rows, slots * rank), lambda i: (0, 0)),
                pl.BlockSpec((slots * rank, block), lambda i: (0, i)),
            ],
            out_specs=pl.BlockSpec((rows, block), lambda i: (0, i)),
            compiler_params=BIG, cost_estimate=cost(13),
        )(masked, weight, back_slots, down_all)
    with jax.named_scope("up_swap"):
        sibling = lax.ppermute(after(square, grad_input), "core", SWAP)
        grad_up = pl.pallas_call(
            spread_kernel,
            out_shape=shape((jobs, rank, value_width), F32),
            in_specs=[SMEM, VMEM, VMEM],
            out_specs=VMEM,
            compiler_params=BIG, cost_estimate=cost(3),
        )(core_at, square, sibling)
    return grad_input, jnp.swapaxes(grad_down, 1, 2), grad_up


def solution(mesh):
    fine = Mesh(mesh.devices.reshape(NY, NCORE, NX, NZ), ("y", "core", "x", "z"))
    dp, tensor, every = ("y", "core"), ("x", "z"), ("y", "core", "x", "z")
    return jax.shard_map(
        body,
        mesh=fine,
        in_specs=(
            P(every, None), P(every, None), P(tensor, None), P(None, tensor, None),
            P(), P(dp, None), P(every), P(every),
        ),
        out_specs=(P(every, None), P(None, tensor, None), P()),
        check_vma=False,
    )
```

```python
import functools
import jax
import jax.numpy as jnp
from jax import lax
from jax.experimental import pallas as pl
from jax.experimental.pallas import tpu as pltpu
from jax.sharding import Mesh, PartitionSpec as P

ADAPTER_SCALING = 2.0
NY, NCORE, NX, NZ = 4, 2, 4, 8
SWAP = [(0, 1), (1, 0)]
PAD = 128
F32, BF16 = jnp.float32, jnp.bfloat16
VMEM = pl.BlockSpec(memory_space=pltpu.VMEM)
SMEM = pl.BlockSpec(memory_space=pltpu.SMEM)
BIG = pltpu.CompilerParams(vmem_limit_bytes=56 * 1024 * 1024)


def cost(microseconds):
    return pl.CostEstimate(flops=0, transcendentals=0, bytes_accessed=int(microseconds * 3_000_000))


def shift(value, axis, size, by):
    return lax.ppermute(value, axis, [(i, (i + by) % size) for i in range(size)])


def after(value, event):
    return lax.optimization_barrier((value, event))[0]


def ring_gather(block, axis, size, me, second=None, last=None):
    rows, columns = block.shape
    half = columns // 2
    whole = jnp.zeros((rows, size * columns), block.dtype)

    def put(whole, piece, owner, offset):
        return lax.dynamic_update_slice(whole, piece, (0, owner * columns + offset))

    whole = put(whole, block, me, 0)
    right = left = block
    for step in range(1, size // 2):
        right = shift(right, axis, size, 1)
        left = shift(left, axis, size, -1)
        whole = put(whole, right, (me - step) % size, 0)
        whole = put(whole, left, (me + step) % size, 0)
        if step == 1 and second is not None:
            right, left = after((right, left), second)
    if last is not None:
        right, left = after((right, left), last)
    far = (me + size // 2) % size
    whole = put(whole, shift(right[:, :half], axis, size, 1), far, 0)
    whole = put(whole, shift(left[:, half:], axis, size, -1), far, half)
    return whole


def tn(a, b):
    return lax.dot_general(a, b, (((0,), (0,)), ((), ())), preferred_element_type=F32)


def nt(a, b):
    return lax.dot_general(a, b, (((1,), (1,)), ((), ())), preferred_element_type=F32)


def nn(a, b):
    return lax.dot_general(a, b, (((1,), (0,)), ((), ())), preferred_element_type=F32)


def back_kernel(x, held, slots, lengths, act, cot, up, masked, back_slots, *terms):
    tiles = slots.shape[0]
    tile_rows = cot.shape[0] // tiles
    rank = up.shape[1]
    span = act.shape[1] // NX
    for tile in range(tiles):
        rows = pl.ds(tile * tile_rows, tile_rows)
        slot = slots[tile]
        row = lax.broadcasted_iota(jnp.int32, (tile_rows, 1), 0)
        live = jnp.where(row < lengths[tile], cot[rows, :], jnp.zeros((), BF16))
        masked[rows, :] = live
        back = nt(live, up[held[0, slot]]).astype(BF16)
        twice = back * jnp.asarray(ADAPTER_SCALING, BF16)
        for s in range(held.shape[1]):
            back_slots[rows, s * rank : (s + 1) * rank] = jnp.where(slot == s, twice, jnp.zeros((), BF16))
        ident = jnp.full((rank, PAD), slot.astype(F32), F32).astype(BF16)
        for by, out in enumerate(terms):
            columns = pl.ds(pl.multiple_of(lax.rem(x[0] + by, NX) * span, span), span)
            out[tile * rank : (tile + 1) * rank, :span] = tn(twice, act[rows, columns]).astype(BF16)
            out[tile * rank : (tile + 1) * rank, span:] = ident


def low_kernel(slots, act, masked, down, out):
    tiles = slots.shape[0]
    tile_rows = act.shape[0] // tiles
    lanes = out.shape[2]
    deep = out.shape[1] // tiles - 8
    rank = NX * deep
    terms, marks = [], []
    for tile in range(tiles):
        rows = pl.ds(tile * tile_rows, tile_rows)
        mine = pl.ds(pl.multiple_of(slots[tile] * rank, rank), rank)
        low = nt(act[rows, :], down[mine, :]).astype(BF16)
        twice = low * jnp.asarray(ADAPTER_SCALING, BF16)
        terms.append(tn(twice, masked[rows, :]).astype(BF16))
        marks.append(jnp.full((8, lanes), slots[tile].astype(F32), F32))
    marks = jnp.concatenate(marks, axis=0).astype(BF16)
    for to_x in range(NX):
        for to_z in range(NZ):
            for tile in range(tiles):
                cut = terms[tile][to_x * deep : (to_x + 1) * deep, to_z * lanes : (to_z + 1) * lanes]
                out[to_x * NZ + to_z, tile * deep : (tile + 1) * deep, :] = cut
            out[to_x * NZ + to_z, tiles * deep :, :] = marks


def up_sum_kernel(tiles, deep, held, downs, parts, out):
    slot_count = held.shape[1]
    lanes = parts.shape[2]
    top = downs.shape[0]
    sums = []
    for slot in range(slot_count):
        total = jnp.zeros((deep, lanes), F32)
        for source in range(parts.shape[0]):
            for tile in range(tiles):
                mark = parts[source, tiles * deep :, :].astype(F32)[tile * 8 : (tile + 1) * 8]
                part = parts[source, tile * deep : (tile + 1) * deep, :].astype(F32)
                total = total + jnp.where(jnp.concatenate([mark] * (deep // 8), axis=0) == slot, part, 0.0)
        sums.append(total)
    sums = jnp.concatenate(sums, axis=0)
    half = sums.shape[0] // 2
    tail = jnp.concatenate([sums[:half], sums[half:]], axis=1)
    tail = jnp.concatenate([tail, jnp.zeros((out.shape[0] - top - half, out.shape[1]), F32)], axis=0)
    row = lax.broadcasted_iota(jnp.int32, tail.shape, 0)
    for s in range(slot_count):
        tail = jnp.where(row == tail.shape[0] - slot_count + s, held[0, s].astype(F32), tail)
    out[:top, :] = downs[...]
    out[top:, :] = tail.astype(BF16)


def slot_kernel(slot_count, tiles, *refs):
    downs, out = refs[:NX], refs[NX]
    rank = downs[0].shape[0] // tiles
    share = out.shape[2]
    span = share * NZ
    idents = [
        [down[tile * rank : (tile + 1) * rank, span : span + PAD].astype(F32) for tile in range(tiles)]
        for down in downs
    ]
    for z in range(NZ):
        for slot in range(slot_count):
            total = jnp.zeros((rank, share), F32)
            for down, ident in zip(downs, idents):
                for tile in range(tiles):
                    part = down[tile * rank : (tile + 1) * rank, z * share : (z + 1) * share].astype(F32)
                    wide = jnp.concatenate([ident[tile] == slot] * (share // PAD), axis=1)
                    total = total + jnp.where(wide, part, 0.0)
            out[z, slot * rank : (slot + 1) * rank, :] = total.astype(BF16)


def share_kernel(parts, out):
    total = parts[0].astype(F32)
    for z in range(1, NZ):
        total = total + parts[z].astype(F32)
    out[...] = total.astype(BF16)


def job_kernel(slot_count, core, ids, parts, down, up, acc):
    jobs, rank, _ = down.shape
    deep = acc.shape[1]
    lanes = acc.shape[2]
    top = slot_count * rank
    half = slot_count * deep // 2
    down[...] = jnp.zeros_like(down)
    acc[...] = jnp.zeros_like(acc)
    for d in range(NY * NCORE):
        tail = parts[d, top:, :].astype(F32)
        ups = jnp.concatenate([tail[:half, :lanes], tail[:half, lanes:]], axis=0)
        for slot in range(slot_count):
            job = ids[d, slot]
            down[job] += parts[d, slot * rank : (slot + 1) * rank, :].astype(F32)
            acc[job] += ups[slot * deep : (slot + 1) * deep, :]
    some = jobs // NCORE
    for i in range(some):
        mine = acc[core[0] * some + i].astype(BF16)
        for copy in range(up.shape[0]):
            up[copy, i * deep : (i + 1) * deep, :] = mine


def spread_kernel(core, mine, other, out):
    some = out.shape[0] // NCORE
    deep = out.shape[1] // NX
    for source, which in ((mine, core[0]), (other, 1 - core[0])):
        for x in range(NX):
            for i in range(some):
                line = [source[x * NZ + z, i * deep : (i + 1) * deep, :] for z in range(NZ)]
                out[which * some + i, x * deep : (x + 1) * deep, :] = jnp.concatenate(line, axis=1).astype(F32)


def input_kernel(masked, weight, back_slots, down, out):
    out[...] = (nt(masked[...], weight[...]) + nn(back_slots[...], down[...])).astype(BF16)


def body(activations, cotangent, frozen_weight, adapter_down, adapter_up, held_jobs, tile_slots, tile_lengths):
    rows, width = activations.shape
    value_width = cotangent.shape[1]
    tiles = tile_slots.shape[0]
    jobs, rank = adapter_up.shape[0], adapter_up.shape[1]
    share = adapter_down.shape[1]
    held = held_jobs[0]
    slots = held.shape[0]
    span = width // NX
    deep = rank // NX
    lanes = value_width // NZ
    some = jobs // NCORE
    shape = jax.ShapeDtypeStruct
    y = lax.axis_index("y")
    core = lax.axis_index("core")
    x = lax.axis_index("x")
    z = lax.axis_index("z")
    core_at, x_at = core.reshape(1), x.reshape(1)

    with jax.named_scope("frozen_gather"):
        part = frozen_weight.shape[0] // (NY * NCORE)
        own_part = lax.dynamic_slice_in_dim(frozen_weight, (y * NCORE + core) * part, part, 0)
        weight = lax.all_gather(own_part, ("x", "z", "y", "core"), axis=0, tiled=True)

    with jax.named_scope("down_terms"):
        masked, back_slots, *down_terms = pl.pallas_call(
            back_kernel,
            out_shape=[shape((rows, value_width), BF16), shape((rows, slots * rank), BF16)]
            + [shape((tiles * rank, span + PAD), BF16)] * NX,
            in_specs=[SMEM] * 4 + [VMEM] * 3,
            out_specs=[VMEM] * (2 + NX),
            compiler_params=BIG, cost_estimate=cost(5.5),
        )(x_at, held_jobs, tile_slots, tile_lengths, activations, cotangent, adapter_up)
    with jax.named_scope("down_x"):
        down_got = [term if by == 0 else shift(term, "x", NX, by) for by, term in enumerate(down_terms)]
    with jax.named_scope("down_sum_x"):
        down_by_z = pl.pallas_call(
            functools.partial(slot_kernel, slots, tiles),
            out_shape=shape((NZ, slots * rank, share), BF16),
            in_specs=[VMEM] * NX,
            out_specs=VMEM,
            compiler_params=BIG, cost_estimate=cost(4),
        )(*down_got)
    with jax.named_scope("down_z"):
        down_from_z = lax.all_to_all(down_by_z, "z", 0, 0, tiled=True)
    with jax.named_scope("down_sum_z"):
        mine = pl.pallas_call(
            share_kernel,
            out_shape=shape((slots * rank, share), BF16),
            in_specs=[VMEM],
            out_specs=VMEM,
            compiler_params=BIG, cost_estimate=cost(2),
        )(down_from_z)
    with jax.named_scope("down_gather"):
        down_mine = jnp.swapaxes(adapter_down, 1, 2)[held].reshape(slots * rank, share)
        down_z = ring_gather(down_mine, "z", NZ, z, second=down_terms)
        down_all = ring_gather(after(down_z, down_got), "x", NX, x)

    with jax.named_scope("up_terms"):
        up_terms = pl.pallas_call(
            low_kernel,
            out_shape=shape((NX * NZ, tiles * (deep + 8), lanes), BF16),
            in_specs=[SMEM] + [VMEM] * 3,
            out_specs=VMEM,
            compiler_params=BIG, cost_estimate=cost(7),
        )(tile_slots, activations, masked, down_all)
    with jax.named_scope("up_tensor"):
        up_got = lax.all_to_all(up_terms, ("x", "z"), 0, 0, tiled=True)
    with jax.named_scope("up_sum"):
        packed = pl.pallas_call(
            functools.partial(up_sum_kernel, tiles, deep),
            out_shape=shape((slots * rank + 32, share), BF16),
            in_specs=[SMEM, VMEM, VMEM],
            out_specs=VMEM,
            compiler_params=BIG, cost_estimate=cost(2),
        )(held_jobs, mine, up_got)
    with jax.named_scope("gather_dp"):
        groups = lax.all_gather(packed, ("y", "core"), axis=0, tiled=False)
        ids = groups[:, slots * rank + 32 - slots :, 0].astype(jnp.int32)
    with jax.named_scope("sum_dp"):
        grad_down, up_copies = pl.pallas_call(
            functools.partial(job_kernel, slots),
            out_shape=[shape((jobs, rank, share), F32), shape((NX * NZ, some * deep, lanes), BF16)],
            in_specs=[SMEM, SMEM, VMEM],
            out_specs=[VMEM, VMEM],
            scratch_shapes=[pltpu.VMEM((jobs, deep, lanes), F32)],
            compiler_params=BIG, cost_estimate=cost(2.5),
        )(core_at, ids, groups)
    with jax.named_scope("up_spread"):
        square = lax.all_to_all(up_copies, ("x", "z"), 0, 0)
    with jax.named_scope("grad_input"):
        block = 2048
        grad_input = pl.pallas_call(
            input_kernel,
            grid=(width // block,),
            out_shape=shape((rows, width), BF16),
            in_specs=[
                pl.BlockSpec((rows, value_width), lambda i: (0, 0)),
                pl.BlockSpec((block, value_width), lambda i: (i, 0)),
                pl.BlockSpec((rows, slots * rank), lambda i: (0, 0)),
                pl.BlockSpec((slots * rank, block), lambda i: (0, i)),
            ],
            out_specs=pl.BlockSpec((rows, block), lambda i: (0, i)),
            compiler_params=BIG, cost_estimate=cost(13),
        )(masked, weight, back_slots, down_all)
    with jax.named_scope("up_swap"):
        sibling = lax.ppermute(after(square, grad_input), "core", SWAP)
        grad_up = pl.pallas_call(
            spread_kernel,
            out_shape=shape((jobs, rank, value_width), F32),
            in_specs=[SMEM, VMEM, VMEM],
            out_specs=VMEM,
            compiler_params=BIG, cost_estimate=cost(3),
        )(core_at, square, sibling)
    return grad_input, jnp.swapaxes(grad_down, 1, 2), grad_up


def solution(mesh):
    fine = Mesh(mesh.devices.reshape(NY, NCORE, NX, NZ), ("y", "core", "x", "z"))
    dp, tensor, every = ("y", "core"), ("x", "z"), ("y", "core", "x", "z")
    return jax.shard_map(
        body,
        mesh=fine,
        in_specs=(
            P(every, None), P(every, None), P(tensor, None), P(None, tensor, None),
            P(), P(dp, None), P(every), P(every),
        ),
        out_specs=(P(every, None), P(None, tensor, None), P()),
        check_vma=False,
    )
```
